1024 devices in a mesh: row: 16 (over y_lo, x, core), col: 32 (over z), seq: 2 (over y_hi).
Axes of the slice: x: 4, y: 4 (y_hi: 2, y_lo: 2; y = y_hi * 2 + y_lo), z: 32, core: 2. Of those that a mesh axis runs over, the one named last changes fastest.
Arguments:
- ffn_input: bfloat16 [1024, 6144], P('seq', 'row'), may hold values from -6 to 6
- attn_mix: bfloat16 [1024, 6144], P('seq', 'col'), may hold values from -6 to 6
- out_grad: bfloat16 [1024, 6144], P('seq', 'row'), may hold values from -6 to 6
- w_gate: bfloat16 [6144, 16384], P('row', 'col'), may hold values from -0.078125 to 0.078125
- w_up: bfloat16 [6144, 16384], P('row', 'col'), may hold values from -0.078125 to 0.078125
- w_down: bfloat16 [6144, 16384], P('row', 'col'), may hold values from -0.046875 to 0.046875
- w_out: bfloat16 [6144, 6144], P('row', 'col'), may hold values from -0.078125 to 0.078125
Outputs:
- resid_grad: bfloat16 [1024, 6144], P('seq', 'row')
- attn_grad: bfloat16 [1024, 6144], P('seq', 'col')
- gate_wgrad: float32 [6144, 16384], P('row', ('col', 'seq'))
- up_wgrad: float32 [6144, 16384], P('row', ('col', 'seq'))
- down_wgrad: float32 [6144, 16384], P('row', ('col', 'seq'))
- out_wgrad: float32 [6144, 6144], P('row', ('col', 'seq'))
The draws below stay inside these ranges and needn't reach their ends.
All inputs are finite; a program needn't handle non-finite values.
Results may differ from the reference program's by a relative error of at most 0.01.
Values may be sent and summed in bfloat16 or wider, within the bound.
No kernel may reach another device: no remote copies, remote signals or barrier semaphores. Data moves between devices by JAX's collectives and lax.ppermute only.
A program may use at most 32 MiB of HBM per device.

```python
import jax
import jax.numpy as jnp

D = 6144
FF = 16384
TOKENS = 1024


def level_of(rng, shape, pieces, low, largest):
    def one(dim, parts):
        heights = jax.random.uniform(jax.random.fold_in(jax.random.fold_in(rng, 6), dim), (parts,), jnp.float32, low / len(pieces), largest / len(pieces))
        return jnp.repeat(jnp.exp(heights), shape[dim] // parts).reshape((-1,) + (1,) * (len(shape) - dim - 1))

    loudness = one(*pieces[0])
    for cut in pieces[1:]:
        loudness = loudness * one(*cut)
    return loudness


def bell_draw(key, shape, deviation, reach, split=(), kind=jnp.bfloat16):
    drawn = deviation * jax.random.normal(key, shape, jnp.float32)
    if split:
        drawn = drawn * level_of(key, shape, split, -0.22, 0.18)
    return jnp.clip(drawn, -reach, reach).astype(kind)


def setup_inputs(seed: int = 0) -> dict:
    seeds = jax.random.split(jax.random.key(seed), 8)
    ffn_input = bell_draw(seeds[0], (TOKENS, D), 1.0, 6.0, ((0, 2), (1, 16)))
    attn_mix = bell_draw(seeds[1], (TOKENS, D), 1.0, 6.0, ((0, 2), (1, 32)))
    out_grad = bell_draw(seeds[2], (TOKENS, D), 1.0, 6.0, ((0, 2), (1, 16)))
    w_gate = bell_draw(seeds[3], (D, FF), D ** -0.5, 0.078125, ((0, 16), (1, 32)))
    w_up = bell_draw(seeds[4], (D, FF), D ** -0.5, 0.078125, ((0, 16), (1, 32)))
    w_down = bell_draw(seeds[5], (D, FF), FF ** -0.5, 0.046875, ((0, 16), (1, 32)))
    w_out = bell_draw(seeds[6], (D, D), D ** -0.5, 0.078125, ((0, 16), (1, 32)))
    return dict(ffn_input=ffn_input, attn_mix=attn_mix, out_grad=out_grad, w_gate=w_gate, w_up=w_up, w_down=w_down, w_out=w_out)


def swiglu_grads(gate_pre, up_pre, hidden_grad):
    sigmoid_gate = jax.nn.sigmoid(gate_pre)
    activated = gate_pre * sigmoid_gate
    hidden = (activated * up_pre).astype(jnp.bfloat16)
    up_grad = (hidden_grad * activated).astype(jnp.bfloat16)
    slope = sigmoid_gate * (1.0 + gate_pre * (1.0 - sigmoid_gate))
    gate_grad = (hidden_grad * up_pre * slope).astype(jnp.bfloat16)
    return gate_grad, up_grad, hidden


def reference(ffn_input, attn_mix, out_grad, w_gate, w_up, w_down, w_out):
    gate_pre = jnp.dot(ffn_input, w_gate, preferred_element_type=jnp.float32)
    up_pre = jnp.dot(ffn_input, w_up, preferred_element_type=jnp.float32)
    hidden_grad = jnp.dot(out_grad, w_down, preferred_element_type=jnp.float32)
    gate_grad, up_grad, hidden = swiglu_grads(gate_pre, up_pre, hidden_grad)
    back_sum = jnp.dot(gate_grad, w_gate.T, preferred_element_type=jnp.float32) + jnp.dot(up_grad, w_up.T, preferred_element_type=jnp.float32)
    resid_grad = (out_grad.astype(jnp.float32) + back_sum).astype(jnp.bfloat16)
    attn_grad = jnp.dot(resid_grad, w_out, preferred_element_type=jnp.float32).astype(jnp.bfloat16)
    norm_factor = TOKENS ** -0.5
    gate_wgrad = jnp.dot(ffn_input.T, gate_grad, preferred_element_type=jnp.float32) * norm_factor
    up_wgrad = jnp.dot(ffn_input.T, up_grad, preferred_element_type=jnp.float32) * norm_factor
    down_wgrad = jnp.dot(out_grad.T, hidden, preferred_element_type=jnp.float32) * norm_factor
    out_wgrad = jnp.dot(resid_grad.T, attn_mix, preferred_element_type=jnp.float32) * norm_factor
    return resid_grad, attn_grad, gate_wgrad, up_wgrad, down_wgrad, out_wgrad
```

```python
import jax
import jax.numpy as jnp
from jax import lax
from jax.sharding import PartitionSpec as P

BF16 = jnp.bfloat16
F32 = jnp.float32


def swiglu_grads(gate_pre, up_pre, hidden_grad):
    sigmoid_gate = jax.nn.sigmoid(gate_pre)
    activated = gate_pre * sigmoid_gate
    hidden = (activated * up_pre).astype(BF16)
    up_grad = (hidden_grad * activated).astype(BF16)
    slope = sigmoid_gate * (1.0 + gate_pre * (1.0 - sigmoid_gate))
    gate_grad = (hidden_grad * up_pre * slope).astype(BF16)
    return (gate_grad, up_grad, hidden)


def dot(first, second):
    return jnp.dot(first, second, preferred_element_type=F32)


def contract_rows(first, second):
    return lax.dot_general(
        first, second, (((0,), (0,)), ((), ())), preferred_element_type=F32
    )


def contract_cols(first, second):
    return lax.dot_general(
        first, second, (((1,), (1,)), ((), ())), preferred_element_type=F32
    )


def scatter_sum(parts, axis, groups):
    got = lax.all_to_all(parts, axis, 0, 0, tiled=True, axis_index_groups=groups)
    return jnp.sum(got.astype(F32), axis=0)


def gather(block, count, axis, groups):
    copies = jnp.broadcast_to(block[None], (count,) + block.shape)
    return lax.all_to_all(copies, axis, 0, 0, tiled=True, axis_index_groups=groups)


def per_device(ffn_input, attn_mix, out_grad, w_gate, w_up, w_down, w_out):
    rows, cols = lax.axis_size("row"), lax.axis_size("col")
    core = lax.axis_index("row") % 2
    seq = lax.axis_index("seq")
    tokens, width = ffn_input.shape
    hidden_width = w_gate.shape[1]
    half = tokens // 2
    chips = rows // 2
    share = half // chips
    core_swap = [(i, i ^ 1) for i in range(rows)]
    seq_swap = [(0, 1), (1, 0)]
    chip_groups = [list(range(c, rows, 2)) for c in range(2)]
    tie = lax.optimization_barrier

    def halves(x):
        mine = lax.dynamic_slice_in_dim(x, core * half, half, 0)
        other = lax.dynamic_slice_in_dim(x, (1 - core) * half, half, 0)
        return mine, other

    in_mine, in_other = halves(ffn_input)
    out_mine, out_other = halves(out_grad)
    acts = lax.ppermute(jnp.concatenate([in_other, out_other]), "row", core_swap)
    weights = lax.ppermute(jnp.concatenate([w_gate, w_up, w_down]), "row", core_swap)
    in_far, out_far = acts[:half], acts[half:]
    gate_far, up_far, down_far = (weights[i * width : (i + 1) * width] for i in range(3))

    def product(x, w, x_far, w_far):
        whole = dot(x, w) + dot(x_far, w_far)
        return whole.astype(BF16).reshape(chips, share, hidden_width)

    parts = jnp.concatenate(
        [
            product(in_mine, w_gate, in_far, gate_far),
            product(in_mine, w_up, in_far, up_far),
            product(out_mine, w_down, out_far, down_far),
        ],
        axis=1,
    )
    parts, w_out_sent = tie((parts, w_out))
    w_out_far = lax.ppermute(w_out_sent, "row", core_swap)
    total = scatter_sum(parts, "row", chip_groups)
    total, w_out_far = tie((total, w_out_far))
    grads = swiglu_grads(total[:share], total[share : 2 * share], total[2 * share :])
    mine = gather(jnp.concatenate(grads, axis=0), chips, "row", chip_groups)

    def split(x):
        return [
            x[:, i * share : (i + 1) * share].reshape(half, hidden_width)
            for i in range(3)
        ]

    gate_mine, up_mine, hid_mine = split(mine)

    near, far = 4, cols // 4

    def place(r, k, j):
        return r * cols + (k * near + j + 2 * (r % 2)) % cols

    near_groups = [[place(r, k, j) for j in range(near)] for r in range(rows) for k in range(far)]
    far_groups = [[place(r, k, j) for k in range(far)] for r in range(rows) for j in range(near)]
    both = ("row", "col")
    spot = (lax.axis_index("col") + cols - 2 * core) % cols
    piece = tokens // cols

    def pair_blocks(own, away):
        return jnp.concatenate([x.reshape(near, half // near, width) for x in (own, away)], axis=1)

    def back(wg, wu):
        return (contract_cols(gate_mine, wg) + contract_cols(up_mine, wu)).astype(BF16)

    back_part = pair_blocks(back(w_gate, w_up), back(gate_far, up_far))
    back_part, mine = tie((back_part, mine))
    other = lax.ppermute(mine, "row", core_swap)
    near_sum = scatter_sum(back_part, both, near_groups).astype(BF16)
    near_sum, other = tie((near_sum, other))
    gate_other, up_other, hid_other = split(other)

    norm_factor = (tokens * lax.axis_size("seq")) ** (-0.5)

    def wgrad(pairs, which):
        size = pairs[0][1].shape[1] // 2
        terms = [
            contract_rows(a, lax.dynamic_slice_in_dim(b, which * size, size, 1))
            for a, b in pairs
        ]
        return sum(terms) * norm_factor

    operands = (
        ((in_mine, gate_mine), (in_other, gate_other)),
        ((in_mine, up_mine), (in_other, up_other)),
        ((out_mine, hid_mine), (out_other, hid_other)),
    )
    sent = jnp.concatenate([wgrad(p, 1 - seq).astype(BF16) for p in operands])
    received = lax.ppermute(sent, "seq", seq_swap)

    far_sum = scatter_sum(near_sum.reshape(far, piece, width), both, far_groups)
    out_all = pair_blocks(out_mine, out_far).reshape(cols, piece, width)
    out_piece = lax.dynamic_index_in_dim(out_all, (spot % near) * far + spot // near, 0, False)
    resid_piece = (out_piece.astype(F32) + far_sum).astype(BF16)
    resid_near = gather(resid_piece, far, both, far_groups).reshape(tokens // near, width)
    resid_near, received = tie((resid_near, received))
    received = received.astype(F32).reshape(3, width, -1)
    wgrads = [wgrad(p, seq) + received[i] for i, p in enumerate(operands)]

    resid_all = gather(resid_near, near, both, near_groups)
    resid_all = resid_all.reshape(near, 2, half // near, width)
    resid_mine, resid_far = (resid_all[:, i].reshape(half, width) for i in range(2))
    mix_part = (dot(resid_mine, w_out) + dot(resid_far, w_out_far)).astype(BF16)
    mix_share = scatter_sum(mix_part.reshape(chips, share, -1), "row", chip_groups)
    mix_all = gather(mix_share.astype(BF16), rows, "row", None)
    attn_grad = mix_all.reshape(chips, 2, share, -1).swapaxes(0, 1).reshape(tokens, -1)

    resid_other = lax.ppermute(resid_far, "row", core_swap)
    resid_grad = jnp.where(
        core == 0,
        jnp.concatenate([resid_mine, resid_other]),
        jnp.concatenate([resid_other, resid_mine]),
    )
    out_pairs = ((resid_grad, attn_mix),)
    out_sent = wgrad(out_pairs, 1 - seq).astype(BF16)
    out_wgrad = wgrad(out_pairs, seq) + lax.ppermute(out_sent, "seq", seq_swap).astype(F32)
    return (resid_grad, attn_grad, *wgrads, out_wgrad)


def solution(mesh):
    return jax.shard_map(
        per_device,
        mesh=mesh,
        in_specs=(
            P("seq", "row"),
            P("seq", "col"),
            P("seq", "row"),
            P("row", "col"),
            P("row", "col"),
            P("row", "col"),
            P("row", "col"),
        ),
        out_specs=(
            P("seq", "row"),
            P("seq", "col"),
            P("row", ("col", "seq")),
            P("row", ("col", "seq")),
            P("row", ("col", "seq")),
            P("row", ("col", "seq")),
        ),
        check_vma=False,
    )
```

```python
import jax
import jax.numpy as jnp
from jax import lax
from jax.sharding import PartitionSpec as P

BF16 = jnp.bfloat16
F32 = jnp.float32


def swiglu_grads(gate_pre, up_pre, hidden_grad):
    sigmoid_gate = jax.nn.sigmoid(gate_pre)
    activated = gate_pre * sigmoid_gate
    hidden = (activated * up_pre).astype(BF16)
    up_grad = (hidden_grad * activated).astype(BF16)
    slope = sigmoid_gate * (1.0 + gate_pre * (1.0 - sigmoid_gate))
    gate_grad = (hidden_grad * up_pre * slope).astype(BF16)
    return (gate_grad, up_grad, hidden)


def dot(first, second):
    return jnp.dot(first, second, preferred_element_type=F32)


def contract_rows(first, second):
    return lax.dot_general(
        first, second, (((0,), (0,)), ((), ())), preferred_element_type=F32
    )


def contract_cols(first, second):
    return lax.dot_general(
        first, second, (((1,), (1,)), ((), ())), preferred_element_type=F32
    )


def scatter_sum(parts, axis, groups):
    got = lax.all_to_all(parts, axis, 0, 0, tiled=True, axis_index_groups=groups)
    return jnp.sum(got.astype(F32), axis=0)


def gather(block, count, axis, groups):
    copies = jnp.broadcast_to(block[None], (count,) + block.shape)
    return lax.all_to_all(copies, axis, 0, 0, tiled=True, axis_index_groups=groups)


def per_device(ffn_input, attn_mix, out_grad, w_gate, w_up, w_down, w_out):
    rows, cols = lax.axis_size("row"), lax.axis_size("col")
    core = lax.axis_index("row") % 2
    seq = lax.axis_index("seq")
    tokens, width = ffn_input.shape
    hidden_width = w_gate.shape[1]
    half = tokens // 2
    chips = rows // 2
    share = half // chips
    core_swap = [(i, i ^ 1) for i in range(rows)]
    seq_swap = [(0, 1), (1, 0)]
    chip_groups = [list(range(c, rows, 2)) for c in range(2)]
    tie = lax.optimization_barrier

    def swap(x):
        return lax.ppermute(x, "row", core_swap)

    def halves(x):
        mine = lax.dynamic_slice_in_dim(x, core * half, half, 0)
        other = lax.dynamic_slice_in_dim(x, (1 - core) * half, half, 0)
        return mine, other

    in_mine, in_other = halves(ffn_input)
    out_mine, out_other = halves(out_grad)

    def products(x, g):
        blocks = [
            dot(a, w).astype(BF16).reshape(chips, share, hidden_width)
            for a, w in ((x, w_gate), (x, w_up), (g, w_down))
        ]
        return jnp.concatenate(blocks, axis=1)

    away = swap(products(in_other, out_other))
    parts = (products(in_mine, out_mine).astype(F32) + away.astype(F32)).astype(BF16)
    parts, *to_swap = tie((parts, w_gate, w_up, w_out, out_other))
    total = scatter_sum(parts, "row", chip_groups)
    total, gate_far, up_far, w_out_far, out_far = tie((total, *(swap(x) for x in to_swap)))
    gate_share, up_share, hid_share = swiglu_grads(
        total[:share], total[share : 2 * share], total[2 * share :]
    )
    hid_all = lax.all_gather(hid_share.astype(F32), "row", axis=0, tiled=True)
    mine = gather(jnp.concatenate([gate_share, up_share]), chips, "row", chip_groups)

    def split(x):
        return [
            x[:, i * share : (i + 1) * share].reshape(half, hidden_width)
            for i in range(2)
        ]

    gate_mine, up_mine = split(mine)

    near, far = 4, cols // 4

    def place(r, k, j):
        return r * cols + (k * near + j + 2 * (r % 2)) % cols

    near_groups = [[place(r, k, j) for j in range(near)] for r in range(rows) for k in range(far)]
    far_groups = [[place(r, k, j) for k in range(far)] for r in range(rows) for j in range(near)]
    both = ("row", "col")
    spot = (lax.axis_index("col") + cols - 2 * core) % cols
    piece = tokens // cols

    def pair_blocks(own, away):
        return jnp.concatenate([x.reshape(near, half // near, width) for x in (own, away)], axis=1)

    def back(wg, wu):
        return (contract_cols(gate_mine, wg) + contract_cols(up_mine, wu)).astype(BF16)

    back_part = pair_blocks(back(w_gate, w_up), back(gate_far, up_far))
    back_part, mine = tie((back_part, mine))
    other = swap(mine)
    near_sum = scatter_sum(back_part, both, near_groups).astype(BF16)
    near_sum, other = tie((near_sum, other))
    gate_other, up_other = split(other)

    norm_factor = (tokens * lax.axis_size("seq")) ** (-0.5)

    def wgrad(pairs, which):
        size = pairs[0][1].shape[1] // 2
        terms = [
            contract_rows(a, lax.dynamic_slice_in_dim(b, which * size, size, 1))
            for a, b in pairs
        ]
        return sum(terms) * norm_factor

    gate_pairs = ((in_mine, gate_mine), (in_other, gate_other))
    up_pairs = ((in_mine, up_mine), (in_other, up_other))
    sent = jnp.concatenate([wgrad(p, 1 - seq).astype(BF16) for p in (gate_pairs, up_pairs)])
    received = lax.ppermute(sent, "seq", seq_swap)

    far_sum = scatter_sum(near_sum.reshape(far, piece, width), both, far_groups)
    far_sum, received, hid_all = tie((far_sum, received, hid_all))
    out_all = pair_blocks(out_mine, out_far).reshape(cols, piece, width)
    out_piece = lax.dynamic_index_in_dim(out_all, (spot % near) * far + spot // near, 0, False)
    resid_piece = (out_piece.astype(F32) + far_sum).astype(BF16)
    out_rows = out_grad.reshape(2, chips, share, width).swapaxes(0, 1).reshape(tokens, width)
    down_pairs = ((out_rows, hid_all.astype(BF16)),)
    down_received = lax.ppermute(wgrad(down_pairs, 1 - seq).astype(BF16), "seq", seq_swap)
    gate_wgrad = wgrad(gate_pairs, seq) + received[:width].astype(F32)
    up_wgrad = wgrad(up_pairs, seq) + received[width:].astype(F32)
    resid_near = gather(resid_piece, far, both, far_groups).reshape(tokens // near, width)
    resid_near, down_received, gate_wgrad, up_wgrad = tie(
        (resid_near, down_received, gate_wgrad, up_wgrad)
    )
    down_wgrad = wgrad(down_pairs, seq) + down_received.astype(F32)

    resid_all = gather(resid_near, near, both, near_groups)
    resid_all, down_wgrad = tie((resid_all, down_wgrad))
    resid_all = resid_all.reshape(near, 2, half // near, width)
    resid_mine, resid_far = (resid_all[:, i].reshape(half, width) for i in range(2))

    def heads_by_tokens(w, x):
        return lax.dot_general(w, x, (((0,), (1,)), ((), ())), preferred_element_type=F32)

    mix_part = (heads_by_tokens(w_out, resid_mine) + heads_by_tokens(w_out_far, resid_far)).astype(BF16)
    mix_part, resid_far = tie((mix_part, resid_far))
    mix_share = scatter_sum(mix_part.reshape(chips, -1, half), "row", chip_groups)
    mix_all = gather(mix_share.astype(BF16), rows, "row", None)
    attn_grad = mix_all.reshape(chips, 2, -1, half).transpose(1, 3, 0, 2).reshape(tokens, -1)

    resid_other = swap(resid_far)
    resid_grad = jnp.where(
        core == 0,
        jnp.concatenate([resid_mine, resid_other]),
        jnp.concatenate([resid_other, resid_mine]),
    )
    out_pairs = ((resid_grad, attn_mix),)
    out_sent = wgrad(out_pairs, 1 - seq).astype(BF16)
    out_wgrad = wgrad(out_pairs, seq) + lax.ppermute(out_sent, "seq", seq_swap).astype(F32)
    return (resid_grad, attn_grad, gate_wgrad, up_wgrad, down_wgrad, out_wgrad)


def solution(mesh):
    return jax.shard_map(
        per_device,
        mesh=mesh,
        in_specs=(
            P("seq", "row"),
            P("seq", "col"),
            P("seq", "row"),
            P("row", "col"),
            P("row", "col"),
            P("row", "col"),
            P("row", "col"),
        ),
        out_specs=(
            P("seq", "row"),
            P("seq", "col"),
            P("row", ("col", "seq")),
            P("row", ("col", "seq")),
            P("row", ("col", "seq")),
            P("row", ("col", "seq")),
        ),
        check_vma=False,
    )
```

```python
import jax
import jax.numpy as jnp
from jax import lax
from jax.sharding import PartitionSpec as P

BF16 = jnp.bfloat16
F32 = jnp.float32


def swiglu_grads(gate_pre, up_pre, hidden_grad):
    sigmoid_gate = jax.nn.sigmoid(gate_pre)
    activated = gate_pre * sigmoid_gate
    hidden = activated * up_pre
    up_grad = (hidden_grad * activated).astype(BF16)
    slope = sigmoid_gate * (1.0 + gate_pre * (1.0 - sigmoid_gate))
    gate_grad = (hidden_grad * up_pre * slope).astype(BF16)
    return (gate_grad, up_grad, hidden)


def dot(first, second):
    return jnp.dot(first, second, preferred_element_type=F32)


def contract_rows(first, second):
    return lax.dot_general(
        first, second, (((0,), (0,)), ((), ())), preferred_element_type=F32
    )


def contract_cols(first, second):
    return lax.dot_general(
        first, second, (((1,), (1,)), ((), ())), preferred_element_type=F32
    )


def scatter_sum(parts, axis, groups):
    got = lax.all_to_all(parts, axis, 0, 0, tiled=True, axis_index_groups=groups)
    return jnp.sum(got.astype(F32), axis=0)


def gather(block, count, axis, groups):
    copies = jnp.broadcast_to(block[None], (count,) + block.shape)
    return lax.all_to_all(copies, axis, 0, 0, tiled=True, axis_index_groups=groups)


def per_device(ffn_input, attn_mix, out_grad, w_gate, w_up, w_down, w_out):
    rows, cols = lax.axis_size("row"), lax.axis_size("col")
    core = lax.axis_index("row") % 2
    seq = lax.axis_index("seq")
    tokens, width = ffn_input.shape
    hidden_width = w_gate.shape[1]
    half = tokens // 2
    chips = rows // 2
    share = half // chips
    core_swap = [(i, i ^ 1) for i in range(rows)]
    seq_swap = [(0, 1), (1, 0)]
    chip_groups = [list(range(c, rows, 2)) for c in range(2)]
    tie = lax.optimization_barrier

    def swap(x):
        return lax.ppermute(x, "row", core_swap)

    def halves(x):
        mine = lax.dynamic_slice_in_dim(x, core * half, half, 0)
        other = lax.dynamic_slice_in_dim(x, (1 - core) * half, half, 0)
        return mine, other

    in_mine, in_other = halves(ffn_input)
    out_mine, out_other = halves(out_grad)

    def products(x, g):
        blocks = [
            dot(a, w).astype(BF16).reshape(chips, share, hidden_width)
            for a, w in ((x, w_gate), (x, w_up), (g, w_down))
        ]
        return jnp.concatenate(blocks, axis=1)

    away = swap(products(in_other, out_other))
    parts = (products(in_mine, out_mine).astype(F32) + away.astype(F32)).astype(BF16)
    parts, *to_swap = tie((parts, w_gate, w_up, w_out, out_other))
    total = scatter_sum(parts, "row", chip_groups)
    total, gate_far, up_far, w_out_far, out_far = tie((total, *(swap(x) for x in to_swap)))
    gate_share, up_share, hid_share = swiglu_grads(
        total[:share], total[share : 2 * share], total[2 * share :]
    )
    mine = gather(jnp.concatenate([gate_share, up_share]), chips, "row", chip_groups)
    mine, hid_share = tie((mine, hid_share))
    hid_all = lax.all_gather(hid_share, "row", axis=0, tiled=True)

    def split(x):
        return [
            x[:, i * share : (i + 1) * share].reshape(half, hidden_width)
            for i in range(2)
        ]

    gate_mine, up_mine = split(mine)

    near, far = 8, cols // 8

    def place(r, k, j):
        return r * cols + (k * near + j + 4 * (r % 2)) % cols

    near_groups = [[place(r, k, j) for j in range(near)] for r in range(rows) for k in range(far)]
    far_groups = [[place(r, k, j) for k in range(far)] for r in range(rows) for j in range(near)]
    both = ("row", "col")
    spot = (lax.axis_index("col") + cols - 4 * core) % near
    piece = tokens // near

    def pair_blocks(own, away):
        return jnp.concatenate([x.reshape(near, half // near, width) for x in (own, away)], axis=1)

    def back(wg, wu):
        return (contract_cols(gate_mine, wg) + contract_cols(up_mine, wu)).astype(BF16)

    back_part = pair_blocks(back(w_gate, w_up), back(gate_far, up_far))
    back_part, mine = tie((back_part, mine))
    other = swap(mine)
    near_sum = scatter_sum(back_part, both, near_groups).astype(BF16)
    near_sum, other = tie((near_sum, other))
    gate_other, up_other = split(other)

    norm_factor = (tokens * lax.axis_size("seq")) ** (-0.5)

    def wgrad(pairs, which, factor=norm_factor):
        size = pairs[0][1].shape[1] // 2
        terms = [
            contract_rows(a, lax.dynamic_slice_in_dim(b, which * size, size, 1))
            for a, b in pairs
        ]
        return sum(terms) * factor

    gate_pairs = ((in_mine, gate_mine), (in_other, gate_other))
    up_pairs = ((in_mine, up_mine), (in_other, up_other))
    sent = jnp.concatenate([wgrad(p, 1 - seq).astype(BF16) for p in (gate_pairs, up_pairs)])
    received = lax.ppermute(sent, "seq", seq_swap)

    group_sums = gather(near_sum, far, both, far_groups)
    far_sum = jnp.sum(group_sums.astype(F32), axis=0)
    far_sum, received, hid_all = tie((far_sum, received, hid_all))
    out_piece = lax.dynamic_index_in_dim(pair_blocks(out_mine, out_far), spot, 0, False)
    resid_piece = (out_piece.astype(F32) + far_sum).astype(BF16)
    out_rows = out_grad.reshape(2, chips, share, width).swapaxes(0, 1).reshape(tokens, width)
    down_pairs = ((out_rows, (hid_all * norm_factor).astype(BF16)),)
    down_received = lax.ppermute(wgrad(down_pairs, 1 - seq, 1.0).astype(BF16), "seq", seq_swap)
    gate_wgrad = wgrad(gate_pairs, seq) + received[:width].astype(F32)
    up_wgrad = wgrad(up_pairs, seq) + received[width:].astype(F32)
    resid_all = gather(resid_piece, near, both, near_groups)
    resid_all, down_received, gate_wgrad, up_wgrad = tie(
        (resid_all, down_received, gate_wgrad, up_wgrad)
    )
    down_wgrad = wgrad(down_pairs, seq, 1.0) + down_received.astype(F32)
    resid_all = resid_all.reshape(near, 2, half // near, width)
    resid_mine, resid_far = (resid_all[:, i].reshape(half, width) for i in range(2))

    def heads_by_tokens(w, x):
        return lax.dot_general(w, x, (((0,), (1,)), ((), ())), preferred_element_type=F32)

    mix_part = (heads_by_tokens(w_out, resid_mine) + heads_by_tokens(w_out_far, resid_far)).astype(BF16)
    mix_part, resid_far = tie((mix_part, resid_far))
    mix_share = scatter_sum(mix_part.reshape(chips, -1, half), "row", chip_groups)
    mix_all = gather(mix_share.astype(BF16), rows, "row", None)
    attn_grad = mix_all.reshape(chips, 2, -1, half).transpose(1, 3, 0, 2).reshape(tokens, -1)

    resid_other = swap(resid_far)
    resid_grad = jnp.where(
        core == 0,
        jnp.concatenate([resid_mine, resid_other]),
        jnp.concatenate([resid_other, resid_mine]),
    )
    out_pairs = ((resid_grad, attn_mix),)
    out_sent = wgrad(out_pairs, 1 - seq).astype(BF16)
    out_wgrad = wgrad(out_pairs, seq) + lax.ppermute(out_sent, "seq", seq_swap).astype(F32)
    return (resid_grad, attn_grad, gate_wgrad, up_wgrad, down_wgrad, out_wgrad)


def solution(mesh):
    return jax.shard_map(
        per_device,
        mesh=mesh,
        in_specs=(
            P("seq", "row"),
            P("seq", "col"),
            P("seq", "row"),
            P("row", "col"),
            P("row", "col"),
            P("row", "col"),
            P("row", "col"),
        ),
        out_specs=(
            P("seq", "row"),
            P("seq", "col"),
            P("row", ("col", "seq")),
            P("row", ("col", "seq")),
            P("row", ("col", "seq")),
            P("row", ("col", "seq")),
        ),
        check_vma=False,
    )
```

```python
import jax
import jax.numpy as jnp
from jax import lax
from jax.sharding import PartitionSpec as P

BF16 = jnp.bfloat16
F32 = jnp.float32


def swiglu_grads(gate_pre, up_pre, hidden_grad):
    sigmoid_gate = jax.nn.sigmoid(gate_pre)
    activated = gate_pre * sigmoid_gate
    hidden = (activated * up_pre).astype(BF16)
    up_grad = (hidden_grad * activated).astype(BF16)
    slope = sigmoid_gate * (1.0 + gate_pre * (1.0 - sigmoid_gate))
    gate_grad = (hidden_grad * up_pre * slope).astype(BF16)
    return (gate_grad, up_grad, hidden)


def dot(first, second):
    return jnp.dot(first, second, preferred_element_type=F32)


def contract_rows(first, second):
    return lax.dot_general(
        first, second, (((0,), (0,)), ((), ())), preferred_element_type=F32
    )


def contract_cols(first, second):
    return lax.dot_general(
        first, second, (((1,), (1,)), ((), ())), preferred_element_type=F32
    )


def scatter_sum(parts, axis, groups):
    got = lax.all_to_all(parts, axis, 0, 0, tiled=True, axis_index_groups=groups)
    return jnp.sum(got.astype(F32), axis=0)


def gather(block, count, axis, groups):
    copies = jnp.broadcast_to(block[None], (count,) + block.shape)
    return lax.all_to_all(copies, axis, 0, 0, tiled=True, axis_index_groups=groups)


def per_device(ffn_input, attn_mix, out_grad, w_gate, w_up, w_down, w_out):
    rows, cols = lax.axis_size("row"), lax.axis_size("col")
    core = lax.axis_index("row") % 2
    seq = lax.axis_index("seq")
    tokens, width = ffn_input.shape
    hidden_width = w_gate.shape[1]
    half = tokens // 2
    chips = rows // 2
    share = half // chips
    core_swap = [(i, i ^ 1) for i in range(rows)]
    seq_swap = [(0, 1), (1, 0)]
    chip_groups = [list(range(c, rows, 2)) for c in range(2)]
    tie = lax.optimization_barrier

    def swap(x):
        return lax.ppermute(x, "row", core_swap)

    def halves(x):
        mine = lax.dynamic_slice_in_dim(x, core * half, half, 0)
        other = lax.dynamic_slice_in_dim(x, (1 - core) * half, half, 0)
        return mine, other

    in_mine, in_other = halves(ffn_input)
    out_mine, out_other = halves(out_grad)

    def products(x, g):
        blocks = [
            dot(a, w).astype(BF16).reshape(chips, share, hidden_width)
            for a, w in ((x, w_gate), (x, w_up), (g, w_down))
        ]
        return jnp.concatenate(blocks, axis=1)

    away = swap(products(in_other, out_other))
    parts = (products(in_mine, out_mine).astype(F32) + away.astype(F32)).astype(BF16)
    parts, *to_swap = tie((parts, w_gate, w_up, w_out, out_other))
    total = scatter_sum(parts, "row", chip_groups)
    total, gate_far, up_far, w_out_far, out_far = tie((total, *(swap(x) for x in to_swap)))
    gate_share, up_share, hid_share = swiglu_grads(
        total[:share], total[share : 2 * share], total[2 * share :]
    )
    mine = gather(jnp.concatenate([gate_share, up_share]), chips, "row", chip_groups)

    def split(x):
        return [
            x[:, i * share : (i + 1) * share].reshape(half, hidden_width)
            for i in range(2)
        ]

    gate_mine, up_mine = split(mine)

    near, far = 8, cols // 8

    def place(r, k, j):
        return r * cols + (k * near + j + 4 * (r % 2)) % cols

    near_groups = [[place(r, k, j) for j in range(near)] for r in range(rows) for k in range(far)]
    far_groups = [[place(r, k, j) for k in range(far)] for r in range(rows) for j in range(near)]
    both = ("row", "col")
    spot = (lax.axis_index("col") + cols - 4 * core) % near
    piece = tokens // near

    def pair_blocks(own, away):
        return jnp.concatenate([x.reshape(near, half // near, width) for x in (own, away)], axis=1)

    def back(wg, wu):
        return (contract_cols(gate_mine, wg) + contract_cols(up_mine, wu)).astype(BF16)

    back_part = pair_blocks(back(w_gate, w_up), back(gate_far, up_far))
    def double(x, bit):
        got = lax.ppermute(x, "row", [(i, i ^ bit) for i in range(rows)])
        low = (lax.axis_index("row") & bit) == 0
        return jnp.where(low, jnp.concatenate([x, got]), jnp.concatenate([got, x]))

    back_part, mine, hid_share = tie((back_part, mine, hid_share))
    other = swap(mine)
    hid_row = double(double(hid_share, 2), 4)
    near_sum = scatter_sum(back_part, both, near_groups).astype(BF16)
    near_sum, other, hid_row = tie((near_sum, other, hid_row))
    gate_other, up_other = split(other)

    norm_factor = (tokens * lax.axis_size("seq")) ** (-0.5)

    def wgrad(pairs, which):
        size = pairs[0][1].shape[1] // 2
        terms = [
            contract_rows(a, lax.dynamic_slice_in_dim(b, which * size, size, 1))
            for a, b in pairs
        ]
        return sum(terms) * norm_factor

    gate_pairs = ((in_mine, gate_mine), (in_other, gate_other))
    up_pairs = ((in_mine, up_mine), (in_other, up_other))
    sent = jnp.concatenate([wgrad(p, 1 - seq).astype(BF16) for p in (gate_pairs, up_pairs)])
    received = lax.ppermute(sent, "seq", seq_swap)
    hid_row, _ = tie((hid_row, sent))
    hid_all = double(double(hid_row, 8), 1)

    group_sums = gather(near_sum, far, both, far_groups)
    far_sum = jnp.sum(group_sums.astype(F32), axis=0)
    far_sum, received, hid_all = tie((far_sum, received, hid_all))
    out_piece = lax.dynamic_index_in_dim(pair_blocks(out_mine, out_far), spot, 0, False)
    resid_piece = (out_piece.astype(F32) + far_sum).astype(BF16)
    down_pairs = ((out_grad, hid_all),)
    down_received = lax.ppermute(wgrad(down_pairs, 1 - seq).astype(BF16), "seq", seq_swap)
    gate_wgrad = wgrad(gate_pairs, seq) + received[:width].astype(F32)
    up_wgrad = wgrad(up_pairs, seq) + received[width:].astype(F32)
    resid_all = gather(resid_piece, near, both, near_groups)
    resid_all, down_received, gate_wgrad, up_wgrad = tie(
        (resid_all, down_received, gate_wgrad, up_wgrad)
    )
    down_wgrad = wgrad(down_pairs, seq) + down_received.astype(F32)
    resid_all = resid_all.reshape(near, 2, half // near, width)
    resid_mine, resid_far = (resid_all[:, i].reshape(half, width) for i in range(2))

    def heads_by_tokens(w, x):
        return lax.dot_general(w, x, (((0,), (1,)), ((), ())), preferred_element_type=F32)

    mix_part = (heads_by_tokens(w_out, resid_mine) + heads_by_tokens(w_out_far, resid_far)).astype(BF16)
    mix_part, resid_far = tie((mix_part, resid_far))
    mix_share = scatter_sum(mix_part.reshape(chips, -1, half), "row", chip_groups)
    mix_all = gather(mix_share.astype(BF16), rows, "row", None)
    attn_grad = mix_all.reshape(chips, 2, -1, half).transpose(1, 3, 0, 2).reshape(tokens, -1)

    resid_other = swap(resid_far)
    resid_grad = jnp.where(
        core == 0,
        jnp.concatenate([resid_mine, resid_other]),
        jnp.concatenate([resid_other, resid_mine]),
    )
    out_pairs = ((resid_grad, attn_mix),)
    out_sent = wgrad(out_pairs, 1 - seq).astype(BF16)
    out_wgrad = wgrad(out_pairs, seq) + lax.ppermute(out_sent, "seq", seq_swap).astype(F32)
    return (resid_grad, attn_grad, gate_wgrad, up_wgrad, down_wgrad, out_wgrad)


def solution(mesh):
    return jax.shard_map(
        per_device,
        mesh=mesh,
        in_specs=(
            P("seq", "row"),
            P("seq", "col"),
            P("seq", "row"),
            P("row", "col"),
            P("row", "col"),
            P("row", "col"),
            P("row", "col"),
        ),
        out_specs=(
            P("seq", "row"),
            P("seq", "col"),
            P("row", ("col", "seq")),
            P("row", ("col", "seq")),
            P("row", ("col", "seq")),
            P("row", ("col", "seq")),
        ),
        check_vma=False,
    )
```

```python
import jax
import jax.numpy as jnp
from jax import lax
from jax.sharding import PartitionSpec as P

BF16 = jnp.bfloat16
F32 = jnp.float32


def swiglu_grads(gate_pre, up_pre, hidden_grad):
    sigmoid_gate = jax.nn.sigmoid(gate_pre)
    activated = gate_pre * sigmoid_gate
    hidden = (activated * up_pre).astype(BF16)
    up_grad = (hidden_grad * activated).astype(BF16)
    slope = sigmoid_gate * (1.0 + gate_pre * (1.0 - sigmoid_gate))
    gate_grad = (hidden_grad * up_pre * slope).astype(BF16)
    return (gate_grad, up_grad, hidden)


def dot(first, second):
    return jnp.dot(first, second, preferred_element_type=F32)


def contract_rows(first, second):
    return lax.dot_general(
        first, second, (((0,), (0,)), ((), ())), preferred_element_type=F32
    )


def contract_cols(first, second):
    return lax.dot_general(
        first, second, (((1,), (1,)), ((), ())), preferred_element_type=F32
    )


def scatter_sum(parts, axis, groups):
    got = lax.all_to_all(parts, axis, 0, 0, tiled=True, axis_index_groups=groups)
    return jnp.sum(got.astype(F32), axis=0)


def gather(block, count, axis, groups):
    copies = jnp.broadcast_to(block[None], (count,) + block.shape)
    return lax.all_to_all(copies, axis, 0, 0, tiled=True, axis_index_groups=groups)


def per_device(ffn_input, attn_mix, out_grad, w_gate, w_up, w_down, w_out):
    rows, cols = lax.axis_size("row"), lax.axis_size("col")
    core = lax.axis_index("row") % 2
    seq = lax.axis_index("seq")
    tokens, width = ffn_input.shape
    hidden_width = w_gate.shape[1]
    half = tokens // 2
    chips = rows // 2
    share = half // chips
    core_swap = [(i, i ^ 1) for i in range(rows)]
    seq_swap = [(0, 1), (1, 0)]
    chip_groups = [list(range(c, rows, 2)) for c in range(2)]
    tie = lax.optimization_barrier

    def swap(x):
        return lax.ppermute(x, "row", core_swap)

    def halves(x):
        mine = lax.dynamic_slice_in_dim(x, core * half, half, 0)
        other = lax.dynamic_slice_in_dim(x, (1 - core) * half, half, 0)
        return mine, other

    in_mine, in_other = halves(ffn_input)
    out_mine, out_other = halves(out_grad)

    def products(x, g):
        blocks = [
            dot(a, w).astype(BF16).reshape(chips, share, hidden_width)
            for a, w in ((x, w_gate), (x, w_up), (g, w_down))
        ]
        return jnp.concatenate(blocks, axis=1)

    away = swap(products(in_other, out_other))
    parts = (products(in_mine, out_mine).astype(F32) + away.astype(F32)).astype(BF16)
    parts, *to_swap = tie((parts, w_gate, w_up, w_out, out_other))
    total = scatter_sum(parts, "row", chip_groups)
    total, gate_far, up_far, w_out_far, out_far = tie((total, *(swap(x) for x in to_swap)))
    gate_share, up_share, hid_share = swiglu_grads(
        total[:share], total[share : 2 * share], total[2 * share :]
    )
    mine = gather(jnp.concatenate([gate_share, up_share]), chips, "row", chip_groups)

    def split(x):
        return [
            x[:, i * share : (i + 1) * share].reshape(half, hidden_width)
            for i in range(2)
        ]

    gate_mine, up_mine = split(mine)

    near, far = 8, cols // 8

    def place(r, k, j):
        return r * cols + (k * near + j + 4 * (r % 2)) % cols

    near_groups = [[place(r, k, j) for j in range(near)] for r in range(rows) for k in range(far)]
    far_groups = [[place(r, k, j) for k in range(far)] for r in range(rows) for j in range(near)]
    both = ("row", "col")
    spot = (lax.axis_index("col") + cols - 4 * core) % near
    piece = tokens // near

    def pair_blocks(own, away):
        return jnp.concatenate([x.reshape(near, half // near, width) for x in (own, away)], axis=1)

    def back(wg, wu):
        return (contract_cols(gate_mine, wg) + contract_cols(up_mine, wu)).astype(BF16)

    back_part = pair_blocks(back(w_gate, w_up), back(gate_far, up_far))
    def double(x, bit):
        got = lax.ppermute(x, "row", [(i, i ^ bit) for i in range(rows)])
        low = (lax.axis_index("row") & bit) == 0
        return jnp.where(low, jnp.concatenate([x, got]), jnp.concatenate([got, x]))

    back_part, mine, hid_share = tie((back_part, mine, hid_share))
    mine, hid_pair = tie((mine, double(hid_share, 2)))
    other = swap(mine)
    hid_row = double(hid_pair, 4)
    near_sum = scatter_sum(back_part, both, near_groups).astype(BF16)
    near_sum, other, hid_row = tie((near_sum, other, hid_row))
    gate_other, up_other = split(other)

    norm_factor = (tokens * lax.axis_size("seq")) ** (-0.5)

    def wgrad(pairs, which):
        size = pairs[0][1].shape[1] // 2
        terms = [
            contract_rows(a, lax.dynamic_slice_in_dim(b, which * size, size, 1))
            for a, b in pairs
        ]
        return sum(terms) * norm_factor

    gate_pairs = ((in_mine, gate_mine), (in_other, gate_other))
    up_pairs = ((in_mine, up_mine), (in_other, up_other))
    sent = jnp.concatenate([wgrad(p, 1 - seq).astype(BF16) for p in (gate_pairs, up_pairs)])
    received = lax.ppermute(sent, "seq", seq_swap)
    hid_row, _ = tie((hid_row, sent))
    hid_chips, received = tie((double(hid_row, 8), received))
    hid_all = double(hid_chips, 1)

    group_sums = gather(near_sum, far, both, far_groups)
    far_sum = jnp.sum(group_sums.astype(F32), axis=0)
    far_sum, hid_all = tie((far_sum, hid_all))
    out_piece = lax.dynamic_index_in_dim(pair_blocks(out_mine, out_far), spot, 0, False)
    resid_piece = (out_piece.astype(F32) + far_sum).astype(BF16)
    down_pairs = ((out_grad, hid_all),)
    down_received = lax.ppermute(wgrad(down_pairs, 1 - seq).astype(BF16), "seq", seq_swap)
    gate_wgrad = wgrad(gate_pairs, seq) + received[:width].astype(F32)
    up_wgrad = wgrad(up_pairs, seq) + received[width:].astype(F32)
    resid_all = gather(resid_piece, near, both, near_groups)
    resid_all, down_received, gate_wgrad, up_wgrad = tie(
        (resid_all, down_received, gate_wgrad, up_wgrad)
    )
    down_wgrad = wgrad(down_pairs, seq) + down_received.astype(F32)
    resid_all = resid_all.reshape(near, 2, half // near, width)
    resid_mine, resid_far = (resid_all[:, i].reshape(half, width) for i in range(2))

    def heads_by_tokens(w, x):
        return lax.dot_general(w, x, (((0,), (1,)), ((), ())), preferred_element_type=F32)

    mix_part = (heads_by_tokens(w_out, resid_mine) + heads_by_tokens(w_out_far, resid_far)).astype(BF16)
    mix_part, resid_far = tie((mix_part, resid_far))
    mix_share = scatter_sum(mix_part.reshape(chips, -1, half), "row", chip_groups)
    mix_share, down_wgrad = tie((mix_share.astype(BF16), down_wgrad))
    mix_all = gather(mix_share, rows, "row", None)
    attn_grad = mix_all.reshape(chips, 2, -1, half).transpose(1, 3, 0, 2).reshape(tokens, -1)

    resid_other = swap(resid_far)
    resid_grad = jnp.where(
        core == 0,
        jnp.concatenate([resid_mine, resid_other]),
        jnp.concatenate([resid_other, resid_mine]),
    )
    out_pairs = ((resid_grad, attn_mix),)
    out_sent = wgrad(out_pairs, 1 - seq).astype(BF16)
    out_wgrad = wgrad(out_pairs, seq) + lax.ppermute(out_sent, "seq", seq_swap).astype(F32)
    return (resid_grad, attn_grad, gate_wgrad, up_wgrad, down_wgrad, out_wgrad)


def solution(mesh):
    return jax.shard_map(
        per_device,
        mesh=mesh,
        in_specs=(
            P("seq", "row"),
            P("seq", "col"),
            P("seq", "row"),
            P("row", "col"),
            P("row", "col"),
            P("row", "col"),
            P("row", "col"),
        ),
        out_specs=(
            P("seq", "row"),
            P("seq", "col"),
            P("row", ("col", "seq")),
            P("row", ("col", "seq")),
            P("row", ("col", "seq")),
            P("row", ("col", "seq")),
        ),
        check_vma=False,
    )
```

```python
import jax
import jax.numpy as jnp
from jax import lax
from jax.sharding import PartitionSpec as P

BF16 = jnp.bfloat16
F32 = jnp.float32


def swiglu_grads(gate_pre, up_pre, hidden_grad):
    sigmoid_gate = jax.nn.sigmoid(gate_pre)
    activated = gate_pre * sigmoid_gate
    hidden = (activated * up_pre).astype(BF16)
    up_grad = (hidden_grad * activated).astype(BF16)
    slope = sigmoid_gate * (1.0 + gate_pre * (1.0 - sigmoid_gate))
    gate_grad = (hidden_grad * up_pre * slope).astype(BF16)
    return (gate_grad, up_grad, hidden)


def dot(first, second):
    return jnp.dot(first, second, preferred_element_type=F32)


def contract_rows(first, second):
    return lax.dot_general(
        first, second, (((0,), (0,)), ((), ())), preferred_element_type=F32
    )


def contract_cols(first, second):
    return lax.dot_general(
        first, second, (((1,), (1,)), ((), ())), preferred_element_type=F32
    )


def scatter_sum(parts, axis, groups):
    got = lax.all_to_all(parts, axis, 0, 0, tiled=True, axis_index_groups=groups)
    return jnp.sum(got.astype(F32), axis=0)


def gather(block, count, axis, groups):
    copies = jnp.broadcast_to(block[None], (count,) + block.shape)
    return lax.all_to_all(copies, axis, 0, 0, tiled=True, axis_index_groups=groups)


def per_device(ffn_input, attn_mix, out_grad, w_gate, w_up, w_down, w_out):
    rows, cols = lax.axis_size("row"), lax.axis_size("col")
    core = lax.axis_index("row") % 2
    seq = lax.axis_index("seq")
    tokens, width = ffn_input.shape
    hidden_width = w_gate.shape[1]
    half = tokens // 2
    chips = rows // 2
    share = half // chips
    core_swap = [(i, i ^ 1) for i in range(rows)]
    seq_swap = [(0, 1), (1, 0)]
    chip_groups = [list(range(c, rows, 2)) for c in range(2)]
    tie = lax.optimization_barrier

    def swap(x):
        return lax.ppermute(x, "row", core_swap)

    def halves(x):
        mine = lax.dynamic_slice_in_dim(x, core * half, half, 0)
        other = lax.dynamic_slice_in_dim(x, (1 - core) * half, half, 0)
        return mine, other

    in_mine, in_other = halves(ffn_input)
    out_mine, out_other = halves(out_grad)

    def products(x, g):
        blocks = [
            dot(a, w).astype(BF16).reshape(chips, share, hidden_width)
            for a, w in ((x, w_gate), (x, w_up), (g, w_down))
        ]
        return jnp.concatenate(blocks, axis=1)

    away = swap(products(in_other, out_other))
    parts = (products(in_mine, out_mine).astype(F32) + away.astype(F32)).astype(BF16)
    parts, w_gate, w_up, *to_swap = tie((parts, w_gate, w_up, w_out, out_other))
    w_both = jnp.concatenate([w_gate, w_up], axis=1)
    to_swap = [w_both, *to_swap]
    total = scatter_sum(parts, "row", chip_groups)
    w_both_far, w_out_far, out_far = (swap(x) for x in to_swap)
    w_pair = jnp.concatenate([w_both, w_both_far])
    w_out_pair = jnp.concatenate([w_out, w_out_far])
    out_pair = jnp.concatenate([out_mine, out_far], axis=1)
    total, w_pair, w_out_pair, out_pair = tie((total, w_pair, w_out_pair, out_pair))
    gate_share, up_share, hid_share = swiglu_grads(
        total[:share], total[share : 2 * share], total[2 * share :]
    )
    mine = gather(jnp.concatenate([gate_share, up_share], axis=1), chips, "row", chip_groups)
    mine = mine.reshape(half, 2 * hidden_width)

    near, far = 8, cols // 8

    def place(r, k, j):
        return r * cols + (k * near + j + 4 * (r % 2)) % cols

    near_groups = [[place(r, k, j) for j in range(near)] for r in range(rows) for k in range(far)]
    far_groups = [[place(r, k, j) for k in range(far)] for r in range(rows) for j in range(near)]
    both = ("row", "col")
    spot = (lax.axis_index("col") + cols - 4 * core) % near

    back_part = contract_cols(mine, w_pair).astype(BF16).reshape(near, half // near, 2 * width)
    def double(x, bit, runs=1):
        got = lax.ppermute(x, "row", [(i, i ^ bit) for i in range(rows)])
        low = (lax.axis_index("row") & bit) == 0
        x, got = (a.reshape(runs, -1, hidden_width) for a in (x, got))
        pair = jnp.where(low, jnp.concatenate([x, got], axis=1), jnp.concatenate([got, x], axis=1))
        return pair.reshape(-1, hidden_width)

    back_part, sent_mine, hid_share = tie((back_part, mine, hid_share))
    sent_mine, hid_pair = tie((sent_mine, double(hid_share, 2)))
    other = swap(sent_mine)
    hid_row = double(hid_pair, 8)
    near_sum = scatter_sum(back_part, both, near_groups).astype(BF16)
    near_sum, other, hid_row = tie((near_sum, other, hid_row))

    norm_factor = (tokens * lax.axis_size("seq")) ** (-0.5)

    def wgrad(pairs, which, start=0, size=hidden_width // 2):
        terms = [
            contract_rows(a, lax.dynamic_slice_in_dim(b, start + which * size, size, 1))
            for a, b in pairs
        ]
        return sum(terms) * norm_factor

    both_pairs = ((in_mine, mine), (in_other, other))
    sent = jnp.concatenate([wgrad(both_pairs, 1 - seq, n).astype(BF16) for n in (0, hidden_width)])
    received = lax.ppermute(sent, "seq", seq_swap)
    hid_row, _ = tie((hid_row, sent))
    hid_chips, received = tie((double(hid_row, 4, 2), received))
    hid_all = double(hid_chips, 1)

    group_sums = gather(near_sum, far, both, far_groups)
    far_sum = jnp.sum(group_sums.astype(F32), axis=0)
    far_sum, hid_all = tie((far_sum, hid_all))
    out_piece = lax.dynamic_index_in_dim(out_pair.reshape(back_part.shape), spot, 0, False)
    resid_piece = (out_piece.astype(F32) + far_sum).astype(BF16)
    down_pairs = ((out_grad, hid_all),)
    down_received = lax.ppermute(wgrad(down_pairs, 1 - seq).astype(BF16), "seq", seq_swap)
    gate_wgrad = wgrad(both_pairs, seq) + received[:width].astype(F32)
    up_wgrad = wgrad(both_pairs, seq, hidden_width) + received[width:].astype(F32)
    resid_all = gather(resid_piece, near, both, near_groups)
    resid_all, down_received, gate_wgrad, up_wgrad = tie(
        (resid_all, down_received, gate_wgrad, up_wgrad)
    )
    down_wgrad = wgrad(down_pairs, seq) + down_received.astype(F32)
    resid_all = resid_all.reshape(half, 2 * width)
    resid_mine, resid_far = resid_all[:, :width], resid_all[:, width:]

    def heads_by_tokens(w, x):
        return lax.dot_general(w, x, (((0,), (1,)), ((), ())), preferred_element_type=F32)

    mix_part = heads_by_tokens(w_out_pair, resid_all).astype(BF16)
    mix_part, resid_far = tie((mix_part, resid_far))
    mix_share = scatter_sum(mix_part.reshape(chips, -1, half), "row", chip_groups)
    mix_share, down_wgrad = tie((mix_share.astype(BF16), down_wgrad))
    mix_all = gather(mix_share, rows, "row", None)
    attn_grad = mix_all.reshape(chips, 2, -1, half).transpose(1, 3, 0, 2).reshape(tokens, -1)

    resid_other = swap(resid_far)
    resid_grad = jnp.where(
        core == 0,
        jnp.concatenate([resid_mine, resid_other]),
        jnp.concatenate([resid_other, resid_mine]),
    )
    out_pairs = ((resid_grad, attn_mix),)
    heads = attn_mix.shape[1] // 2
    out_sent = wgrad(out_pairs, 1 - seq, 0, heads).astype(BF16)
    out_wgrad = wgrad(out_pairs, seq, 0, heads) + lax.ppermute(out_sent, "seq", seq_swap).astype(F32)
    return (resid_grad, attn_grad, gate_wgrad, up_wgrad, down_wgrad, out_wgrad)


def solution(mesh):
    return jax.shard_map(
        per_device,
        mesh=mesh,
        in_specs=(
            P("seq", "row"),
            P("seq", "col"),
            P("seq", "row"),
            P("row", "col"),
            P("row", "col"),
            P("row", "col"),
            P("row", "col"),
        ),
        out_specs=(
            P("seq", "row"),
            P("seq", "col"),
            P("row", ("col", "seq")),
            P("row", ("col", "seq")),
            P("row", ("col", "seq")),
            P("row", ("col", "seq")),
        ),
        check_vma=False,
    )
```

```python
import jax
import jax.numpy as jnp
from jax import lax
from jax.sharding import PartitionSpec as P

BF16 = jnp.bfloat16
F32 = jnp.float32


def swiglu_grads(gate_pre, up_pre, hidden_grad):
    sigmoid_gate = jax.nn.sigmoid(gate_pre)
    activated = gate_pre * sigmoid_gate
    hidden = (activated * up_pre).astype(BF16)
    up_grad = (hidden_grad * activated).astype(BF16)
    slope = sigmoid_gate * (1.0 + gate_pre * (1.0 - sigmoid_gate))
    gate_grad = (hidden_grad * up_pre * slope).astype(BF16)
    return (gate_grad, up_grad, hidden)


def dot(first, second):
    return jnp.dot(first, second, preferred_element_type=F32)


def contract_rows(first, second):
    return lax.dot_general(
        first, second, (((0,), (0,)), ((), ())), preferred_element_type=F32
    )


def contract_cols(first, second):
    return lax.dot_general(
        first, second, (((1,), (1,)), ((), ())), preferred_element_type=F32
    )


def scatter_sum(parts, axis, groups):
    got = lax.all_to_all(parts, axis, 0, 0, tiled=True, axis_index_groups=groups)
    return jnp.sum(got.astype(F32), axis=0)


def gather(block, count, axis, groups):
    copies = jnp.broadcast_to(block[None], (count,) + block.shape)
    return lax.all_to_all(copies, axis, 0, 0, tiled=True, axis_index_groups=groups)


def per_device(ffn_input, attn_mix, out_grad, w_gate, w_up, w_down, w_out):
    rows, cols = lax.axis_size("row"), lax.axis_size("col")
    core = lax.axis_index("row") % 2
    seq = lax.axis_index("seq")
    tokens, width = ffn_input.shape
    hidden_width = w_gate.shape[1]
    half = tokens // 2
    chips = rows // 2
    share = half // chips
    core_swap = [(i, i ^ 1) for i in range(rows)]
    seq_swap = [(0, 1), (1, 0)]
    chip_groups = [list(range(c, rows, 2)) for c in range(2)]
    tie = lax.optimization_barrier

    def swap(x):
        return lax.ppermute(x, "row", core_swap)

    def halves(x):
        mine = lax.dynamic_slice_in_dim(x, core * half, half, 0)
        other = lax.dynamic_slice_in_dim(x, (1 - core) * half, half, 0)
        return mine, other

    in_mine, in_other = halves(ffn_input)
    out_mine, out_other = halves(out_grad)

    def products(x, g):
        blocks = [
            dot(a, w).astype(BF16).reshape(chips, share, hidden_width)
            for a, w in ((x, w_gate), (x, w_up), (g, w_down))
        ]
        return jnp.concatenate(blocks, axis=1)

    away = swap(products(in_other, out_other))
    parts = (products(in_mine, out_mine).astype(F32) + away.astype(F32)).astype(BF16)
    parts, w_gate, w_up, *to_swap = tie((parts, w_gate, w_up, w_out, out_other))
    w_both = jnp.concatenate([w_gate, w_up], axis=1)
    to_swap = [w_both, *to_swap]
    total = scatter_sum(parts, "row", chip_groups)
    w_both_far, w_out_far, out_far = (swap(x) for x in to_swap)
    w_pair = jnp.concatenate([w_both, w_both_far])
    w_out_pair = jnp.concatenate([w_out, w_out_far])
    out_pair = jnp.concatenate([out_mine, out_far], axis=1)
    total, w_pair, w_out_pair, out_pair = tie((total, w_pair, w_out_pair, out_pair))
    gate_share, up_share, hid_share = swiglu_grads(
        total[:share], total[share : 2 * share], total[2 * share :]
    )
    def double(x, bit, runs=1):
        got = lax.ppermute(x, "row", [(i, i ^ bit) for i in range(rows)])
        low = (lax.axis_index("row") & bit) == 0
        x, got = (a.reshape(runs, -1, hidden_width) for a in (x, got))
        pair = jnp.where(low, jnp.concatenate([x, got], axis=1), jnp.concatenate([got, x], axis=1))
        return pair.reshape(-1, hidden_width)

    mine = gather(jnp.concatenate([gate_share, up_share], axis=1), chips, "row", chip_groups)
    mine, hid_pair = tie((mine.reshape(half, 2 * hidden_width), double(hid_share, 2)))

    near, far = 8, cols // 8

    def place(r, k, j):
        return r * cols + (k * near + j + 4 * (r % 2)) % cols

    near_groups = [[place(r, k, j) for j in range(near)] for r in range(rows) for k in range(far)]
    far_groups = [[place(r, k, j) for k in range(far)] for r in range(rows) for j in range(near)]
    both = ("row", "col")
    spot = (lax.axis_index("col") + cols - 4 * core) % near

    back_part = contract_cols(mine, w_pair).astype(BF16).reshape(near, half // near, 2 * width)
    back_part, sent_mine, hid_pair = tie((back_part, mine, hid_pair))
    other = swap(sent_mine)
    hid_row = double(hid_pair, 8)
    near_sum = scatter_sum(back_part, both, near_groups).astype(BF16)
    near_sum, other, hid_row = tie((near_sum, other, hid_row))

    norm_factor = (tokens * lax.axis_size("seq")) ** (-0.5)

    def wgrad(pairs, which, start=0, size=hidden_width // 2):
        terms = [
            contract_rows(a, lax.dynamic_slice_in_dim(b, start + which * size, size, 1))
            for a, b in pairs
        ]
        return sum(terms) * norm_factor

    both_pairs = ((in_mine, mine), (in_other, other))
    sent = jnp.concatenate([wgrad(both_pairs, 1 - seq, n).astype(BF16) for n in (0, hidden_width)])
    received = lax.ppermute(sent, "seq", seq_swap)
    hid_row, _ = tie((hid_row, sent))
    hid_chips, received = tie((double(hid_row, 4, 2), received))
    hid_all = double(hid_chips, 1)

    group_sums = gather(near_sum, far, both, far_groups)
    far_sum = jnp.sum(group_sums.astype(F32), axis=0)
    gate_wgrad = wgrad(both_pairs, seq) + received[:width].astype(F32)
    up_wgrad = wgrad(both_pairs, seq, hidden_width) + received[width:].astype(F32)
    out_piece = lax.dynamic_index_in_dim(out_pair.reshape(back_part.shape), spot, 0, False)
    far_sum, hid_all, gate_wgrad, up_wgrad, out_piece = tie(
        (far_sum, hid_all, gate_wgrad, up_wgrad, out_piece)
    )
    resid_piece = (out_piece.astype(F32) + far_sum).astype(BF16)
    down_pairs = ((out_grad, hid_all),)
    down_received = lax.ppermute(wgrad(down_pairs, 1 - seq).astype(BF16), "seq", seq_swap)
    resid_all = gather(resid_piece, near, both, near_groups)
    resid_all, down_received = tie((resid_all, down_received))
    down_wgrad = wgrad(down_pairs, seq) + down_received.astype(F32)
    resid_all = resid_all.reshape(half, 2 * width)
    resid_mine, resid_far = resid_all[:, :width], resid_all[:, width:]

    def heads_by_tokens(w, x):
        return lax.dot_general(w, x, (((0,), (1,)), ((), ())), preferred_element_type=F32)

    mix_part = heads_by_tokens(w_out_pair, resid_all).astype(BF16)
    mix_part, resid_far = tie((mix_part, resid_far))
    mix_share = scatter_sum(mix_part.reshape(chips, -1, half), "row", chip_groups)
    mix_share, down_wgrad = tie((mix_share.astype(BF16), down_wgrad))
    mix_all = gather(mix_share, rows, "row", None)
    attn_grad = mix_all.reshape(chips, 2, -1, half).transpose(1, 3, 0, 2).reshape(tokens, -1)

    resid_other = swap(resid_far)
    resid_grad = jnp.where(
        core == 0,
        jnp.concatenate([resid_mine, resid_other]),
        jnp.concatenate([resid_other, resid_mine]),
    )
    out_pairs = ((resid_grad, attn_mix),)
    heads = attn_mix.shape[1] // 2
    out_sent = wgrad(out_pairs, 1 - seq, 0, heads).astype(BF16)
    out_wgrad = wgrad(out_pairs, seq, 0, heads) + lax.ppermute(out_sent, "seq", seq_swap).astype(F32)
    return (resid_grad, attn_grad, gate_wgrad, up_wgrad, down_wgrad, out_wgrad)


def solution(mesh):
    return jax.shard_map(
        per_device,
        mesh=mesh,
        in_specs=(
            P("seq", "row"),
            P("seq", "col"),
            P("seq", "row"),
            P("row", "col"),
            P("row", "col"),
            P("row", "col"),
            P("row", "col"),
        ),
        out_specs=(
            P("seq", "row"),
            P("seq", "col"),
            P("row", ("col", "seq")),
            P("row", ("col", "seq")),
            P("row", ("col", "seq")),
            P("row", ("col", "seq")),
        ),
        check_vma=False,
    )
```

```python
import jax
import jax.numpy as jnp
from jax import lax
from jax.sharding import PartitionSpec as P

BF16 = jnp.bfloat16
F32 = jnp.float32


def swiglu_grads(gate_pre, up_pre, hidden_grad):
    sigmoid_gate = jax.nn.sigmoid(gate_pre)
    activated = gate_pre * sigmoid_gate
    hidden = (activated * up_pre).astype(BF16)
    up_grad = (hidden_grad * activated).astype(BF16)
    slope = sigmoid_gate * (1.0 + gate_pre * (1.0 - sigmoid_gate))
    gate_grad = (hidden_grad * up_pre * slope).astype(BF16)
    return (gate_grad, up_grad, hidden)


def dot(first, second):
    return jnp.dot(first, second, preferred_element_type=F32)


def contract_rows(first, second):
    return lax.dot_general(
        first, second, (((0,), (0,)), ((), ())), preferred_element_type=F32
    )


def contract_cols(first, second):
    return lax.dot_general(
        first, second, (((1,), (1,)), ((), ())), preferred_element_type=F32
    )


def scatter_sum(parts, axis, groups):
    got = lax.all_to_all(parts, axis, 0, 0, tiled=True, axis_index_groups=groups)
    return jnp.sum(got.astype(F32), axis=0)


def gather(block, count, axis, groups):
    copies = jnp.broadcast_to(block[None], (count,) + block.shape)
    return lax.all_to_all(copies, axis, 0, 0, tiled=True, axis_index_groups=groups)


def per_device(ffn_input, attn_mix, out_grad, w_gate, w_up, w_down, w_out):
    rows, cols = lax.axis_size("row"), lax.axis_size("col")
    core = lax.axis_index("row") % 2
    seq = lax.axis_index("seq")
    tokens, width = ffn_input.shape
    hidden_width = w_gate.shape[1]
    half = tokens // 2
    chips = rows // 2
    share = half // chips
    core_swap = [(i, i ^ 1) for i in range(rows)]
    seq_swap = [(0, 1), (1, 0)]
    chip_groups = [list(range(c, rows, 2)) for c in range(2)]
    tie = lax.optimization_barrier
    near, far = 8, cols // 8

    def swap(x):
        return lax.ppermute(x, "row", core_swap)

    def halves(x):
        mine = lax.dynamic_slice_in_dim(x, core * half, half, 0)
        other = lax.dynamic_slice_in_dim(x, (1 - core) * half, half, 0)
        return mine, other

    in_mine, in_other = halves(ffn_input)
    out_mine, out_other = halves(out_grad)

    def products(x, g):
        blocks = [
            dot(a, w).astype(BF16).reshape(chips, share, hidden_width)
            for a, w in ((x, w_gate), (x, w_up), (g, w_down))
        ]
        return jnp.concatenate(blocks, axis=1)

    away = swap(products(in_other, out_other))
    parts = (products(in_mine, out_mine).astype(F32) + away.astype(F32)).astype(BF16)
    parts, w_gate, w_up, *to_swap = tie((parts, w_gate, w_up, w_out, out_other))
    w_both = jnp.concatenate([w_gate, w_up], axis=1)
    to_swap = [w_both, *to_swap]
    total = scatter_sum(parts, "row", chip_groups)
    w_both_far, w_out_far, out_far = (swap(x) for x in to_swap)
    w_pair = jnp.concatenate([w_both, w_both_far])
    w_out_pair = jnp.concatenate([w_out, w_out_far])
    out_pair = jnp.concatenate([out_mine, out_far], axis=1)
    spot = (lax.axis_index("col") + cols - 4 * core) % near
    out_piece = lax.dynamic_index_in_dim(out_pair.reshape(near, half // near, 2 * width), spot, 0, False)
    total, w_out_pair, out_piece = tie((total, w_out_pair, out_piece))
    gate_share, up_share, hid_share = swiglu_grads(
        total[:share], total[share : 2 * share], total[2 * share :]
    )
    def double(x, bit, runs=1):
        got = lax.ppermute(x, "row", [(i, i ^ bit) for i in range(rows)])
        low = (lax.axis_index("row") & bit) == 0
        x, got = (a.reshape(runs, -1, hidden_width) for a in (x, got))
        pair = jnp.where(low, jnp.concatenate([x, got], axis=1), jnp.concatenate([got, x], axis=1))
        return pair.reshape(-1, hidden_width)

    mine = gather(jnp.concatenate([gate_share, up_share], axis=1), chips, "row", chip_groups)
    mine, hid_pair, w_pair = tie(
        (mine.reshape(half, 2 * hidden_width), double(hid_share, 2), w_pair)
    )

    def place(r, k, j):
        return r * cols + (k * near + j + 4 * (r % 2)) % cols

    near_groups = [[place(r, k, j) for j in range(near)] for r in range(rows) for k in range(far)]
    far_groups = [[place(r, k, j) for k in range(far)] for r in range(rows) for j in range(near)]
    both = ("row", "col")

    back_part = contract_cols(mine, w_pair).astype(BF16).reshape(near, half // near, 2 * width)
    back_part, sent_mine, hid_pair = tie((back_part, mine, hid_pair))
    other = swap(sent_mine)
    hid_row = double(hid_pair, 8)
    near_sum = scatter_sum(back_part, both, near_groups).astype(BF16)
    near_sum, other, hid_row = tie((near_sum, other, hid_row))

    norm_factor = (tokens * lax.axis_size("seq")) ** (-0.5)

    def wgrad(pairs, which, start=0, size=hidden_width // 2):
        terms = [
            contract_rows(a, lax.dynamic_slice_in_dim(b, start + which * size, size, 1))
            for a, b in pairs
        ]
        return sum(terms) * norm_factor

    both_pairs = ((in_mine, mine), (in_other, other))
    sent = jnp.concatenate([wgrad(both_pairs, 1 - seq, n).astype(BF16) for n in (0, hidden_width)])
    received = lax.ppermute(sent, "seq", seq_swap)
    hid_row, _ = tie((hid_row, sent))
    hid_chips, received = tie((double(hid_row, 4, 2), received))
    hid_all = double(hid_chips, 1)

    group_sums = gather(near_sum, far, both, far_groups)
    far_sum = jnp.sum(group_sums.astype(F32), axis=0)
    gate_wgrad = wgrad(both_pairs, seq) + received[:width].astype(F32)
    up_wgrad = wgrad(both_pairs, seq, hidden_width) + received[width:].astype(F32)
    far_sum, hid_all, gate_wgrad = tie((far_sum, hid_all, gate_wgrad))
    resid_piece = (out_piece.astype(F32) + far_sum).astype(BF16)
    down_pairs = ((out_grad, hid_all),)
    down_received = lax.ppermute(wgrad(down_pairs, 1 - seq).astype(BF16), "seq", seq_swap)
    resid_all = gather(resid_piece, near, both, near_groups)
    resid_all, down_received, up_wgrad = tie((resid_all, down_received, up_wgrad))
    down_wgrad = wgrad(down_pairs, seq) + down_received.astype(F32)
    resid_all = resid_all.reshape(half, 2 * width)
    resid_mine, resid_far = resid_all[:, :width], resid_all[:, width:]

    def heads_by_tokens(w, x):
        return lax.dot_general(w, x, (((0,), (1,)), ((), ())), preferred_element_type=F32)

    mix_part = heads_by_tokens(w_out_pair, resid_all).astype(BF16)
    mix_part, resid_far = tie((mix_part, resid_far))
    mix_share = scatter_sum(mix_part.reshape(chips, -1, half), "row", chip_groups)
    mix_share, down_wgrad = tie((mix_share.astype(BF16), down_wgrad))
    mix_all = gather(mix_share, rows, "row", None)
    attn_grad = mix_all.reshape(chips, 2, -1, half).transpose(1, 3, 0, 2).reshape(tokens, -1)

    resid_other = swap(resid_far)
    resid_grad = jnp.where(
        core == 0,
        jnp.concatenate([resid_mine, resid_other]),
        jnp.concatenate([resid_other, resid_mine]),
    )
    out_pairs = ((resid_grad, attn_mix),)
    heads = attn_mix.shape[1] // 2
    out_sent = wgrad(out_pairs, 1 - seq, 0, heads).astype(BF16)
    out_wgrad = wgrad(out_pairs, seq, 0, heads) + lax.ppermute(out_sent, "seq", seq_swap).astype(F32)
    return (resid_grad, attn_grad, gate_wgrad, up_wgrad, down_wgrad, out_wgrad)


def solution(mesh):
    return jax.shard_map(
        per_device,
        mesh=mesh,
        in_specs=(
            P("seq", "row"),
            P("seq", "col"),
            P("seq", "row"),
            P("row", "col"),
            P("row", "col"),
            P("row", "col"),
            P("row", "col"),
        ),
        out_specs=(
            P("seq", "row"),
            P("seq", "col"),
            P("row", ("col", "seq")),
            P("row", ("col", "seq")),
            P("row", ("col", "seq")),
            P("row", ("col", "seq")),
        ),
        check_vma=False,
    )
```

```python
import jax
import jax.numpy as jnp
from jax import lax
from jax.sharding import PartitionSpec as P

BF16 = jnp.bfloat16
F32 = jnp.float32


def swiglu_grads(gate_pre, up_pre, hidden_grad):
    sigmoid_gate = jax.nn.sigmoid(gate_pre)
    activated = gate_pre * sigmoid_gate
    hidden = (activated * up_pre).astype(BF16)
    up_grad = (hidden_grad * activated).astype(BF16)
    slope = sigmoid_gate * (1.0 + gate_pre * (1.0 - sigmoid_gate))
    gate_grad = (hidden_grad * up_pre * slope).astype(BF16)
    return (gate_grad, up_grad, hidden)


def dot(first, second):
    return jnp.dot(first, second, preferred_element_type=F32)


def contract_rows(first, second):
    return lax.dot_general(
        first, second, (((0,), (0,)), ((), ())), preferred_element_type=F32
    )


def contract_cols(first, second):
    return lax.dot_general(
        first, second, (((1,), (1,)), ((), ())), preferred_element_type=F32
    )


def scatter_sum(parts, axis, groups):
    got = lax.all_to_all(parts, axis, 0, 0, tiled=True, axis_index_groups=groups)
    return jnp.sum(got.astype(F32), axis=0)


def gather(block, count, axis, groups):
    copies = jnp.broadcast_to(block[None], (count,) + block.shape)
    return lax.all_to_all(copies, axis, 0, 0, tiled=True, axis_index_groups=groups)


def per_device(ffn_input, attn_mix, out_grad, w_gate, w_up, w_down, w_out):
    rows, cols = lax.axis_size("row"), lax.axis_size("col")
    core = lax.axis_index("row") % 2
    seq = lax.axis_index("seq")
    tokens, width = ffn_input.shape
    hidden_width = w_gate.shape[1]
    half = tokens // 2
    chips = rows // 2
    share = half // chips
    core_swap = [(i, i ^ 1) for i in range(rows)]
    seq_swap = [(0, 1), (1, 0)]
    chip_groups = [list(range(c, rows, 2)) for c in range(2)]
    tie = lax.optimization_barrier
    near, far = 8, cols // 8

    def swap(x):
        return lax.ppermute(x, "row", core_swap)

    def halves(x):
        mine = lax.dynamic_slice_in_dim(x, core * half, half, 0)
        other = lax.dynamic_slice_in_dim(x, (1 - core) * half, half, 0)
        return mine, other

    in_mine, in_other = halves(ffn_input)
    out_mine, out_other = halves(out_grad)

    def products(x, g):
        blocks = [
            dot(a, w).astype(BF16).reshape(chips, share, hidden_width)
            for a, w in ((x, w_gate), (x, w_up), (g, w_down))
        ]
        return jnp.concatenate(blocks, axis=1)

    away = swap(products(in_other, out_other))
    parts = (products(in_mine, out_mine).astype(F32) + away.astype(F32)).astype(BF16)
    parts, w_gate, w_up, *to_swap = tie((parts, w_gate, w_up, w_out, out_other))
    w_both = jnp.concatenate([w_gate, w_up], axis=1)
    to_swap = [w_both, *to_swap]
    total = scatter_sum(parts, "row", chip_groups)
    w_both_far, w_out_far, out_far = (swap(x) for x in to_swap)
    w_out_pair = jnp.concatenate([w_out, w_out_far])
    out_pair = jnp.concatenate([out_mine, out_far], axis=1)
    spot = (lax.axis_index("col") + cols - 4 * core) % near
    out_piece = lax.dynamic_index_in_dim(out_pair.reshape(near, half // near, 2 * width), spot, 0, False)
    total, w_both_far, w_out_pair, out_piece = tie((total, w_both_far, w_out_pair, out_piece))
    gate_share, up_share, hid_share = swiglu_grads(
        total[:share], total[share : 2 * share], total[2 * share :]
    )
    def double(x, bit, runs=1):
        got = lax.ppermute(x, "row", [(i, i ^ bit) for i in range(rows)])
        low = (lax.axis_index("row") & bit) == 0
        x, got = (a.reshape(runs, -1, hidden_width) for a in (x, got))
        pair = jnp.where(low, jnp.concatenate([x, got], axis=1), jnp.concatenate([got, x], axis=1))
        return pair.reshape(-1, hidden_width)

    mine = gather(jnp.concatenate([gate_share, up_share], axis=1), chips, "row", chip_groups)
    mine, hid_pair = tie((mine.reshape(half, 2 * hidden_width), double(hid_share, 2)))

    def place(r, k, j):
        return r * cols + (k * near + j + 4 * (r % 2)) % cols

    near_groups = [[place(r, k, j) for j in range(near)] for r in range(rows) for k in range(far)]
    far_groups = [[place(r, k, j) for k in range(far)] for r in range(rows) for j in range(near)]
    both = ("row", "col")

    back_part = jnp.concatenate([contract_cols(mine, w).astype(BF16) for w in (w_both, w_both_far)], axis=1)
    back_part = back_part.reshape(near, half // near, 2 * width)
    back_part, sent_mine, hid_pair = tie((back_part, mine, hid_pair))
    other = swap(sent_mine)
    hid_row = double(hid_pair, 8)
    near_sum = scatter_sum(back_part, both, near_groups).astype(BF16)
    near_sum, other, hid_row = tie((near_sum, other, hid_row))

    norm_factor = (tokens * lax.axis_size("seq")) ** (-0.5)

    def wgrad(pairs, which, start=0, size=hidden_width // 2):
        terms = [
            contract_rows(a, lax.dynamic_slice_in_dim(b, start + which * size, size, 1))
            for a, b in pairs
        ]
        return sum(terms) * norm_factor

    both_pairs = ((in_mine, mine), (in_other, other))
    sent = jnp.concatenate([wgrad(both_pairs, 1 - seq, n).astype(BF16) for n in (0, hidden_width)])
    received = lax.ppermute(sent, "seq", seq_swap)
    hid_row, _ = tie((hid_row, sent))
    hid_chips, received = tie((double(hid_row, 4, 2), received))
    hid_all = double(hid_chips, 1)

    group_sums = gather(near_sum, far, both, far_groups)
    far_sum = jnp.sum(group_sums.astype(F32), axis=0)
    gate_wgrad = wgrad(both_pairs, seq) + received[:width].astype(F32)
    up_wgrad = wgrad(both_pairs, seq, hidden_width) + received[width:].astype(F32)
    far_sum, hid_all = tie((far_sum, hid_all))
    resid_piece = (out_piece.astype(F32) + far_sum).astype(BF16)
    down_pairs = ((out_grad, hid_all),)
    down_received = lax.ppermute(wgrad(down_pairs, 1 - seq).astype(BF16), "seq", seq_swap)
    resid_all = gather(resid_piece, near, both, near_groups)
    resid_all, down_received, gate_wgrad, up_wgrad = tie(
        (resid_all, down_received, gate_wgrad, up_wgrad)
    )
    down_wgrad = wgrad(down_pairs, seq) + down_received.astype(F32)
    resid_all = resid_all.reshape(half, 2 * width)
    resid_mine, resid_far = resid_all[:, :width], resid_all[:, width:]

    def heads_by_tokens(w, x):
        return lax.dot_general(w, x, (((0,), (1,)), ((), ())), preferred_element_type=F32)

    mix_part = heads_by_tokens(w_out_pair, resid_all).astype(BF16)
    mix_part, resid_far = tie((mix_part, resid_far))
    mix_share = scatter_sum(mix_part.reshape(chips, -1, half), "row", chip_groups)
    mix_share, down_wgrad = tie((mix_share.astype(BF16), down_wgrad))
    mix_all = gather(mix_share, rows, "row", None)
    attn_grad = mix_all.reshape(chips, 2, -1, half).transpose(1, 3, 0, 2).reshape(tokens, -1)

    resid_other = swap(resid_far)
    resid_grad = jnp.where(
        core == 0,
        jnp.concatenate([resid_mine, resid_other]),
        jnp.concatenate([resid_other, resid_mine]),
    )
    out_pairs = ((resid_grad, attn_mix),)
    heads = attn_mix.shape[1] // 2
    out_sent = wgrad(out_pairs, 1 - seq, 0, heads).astype(BF16)
    out_wgrad = wgrad(out_pairs, seq, 0, heads) + lax.ppermute(out_sent, "seq", seq_swap).astype(F32)
    return (resid_grad, attn_grad, gate_wgrad, up_wgrad, down_wgrad, out_wgrad)


def solution(mesh):
    return jax.shard_map(
        per_device,
        mesh=mesh,
        in_specs=(
            P("seq", "row"),
            P("seq", "col"),
            P("seq", "row"),
            P("row", "col"),
            P("row", "col"),
            P("row", "col"),
            P("row", "col"),
        ),
        out_specs=(
            P("seq", "row"),
            P("seq", "col"),
            P("row", ("col", "seq")),
            P("row", ("col", "seq")),
            P("row", ("col", "seq")),
            P("row", ("col", "seq")),
        ),
        check_vma=False,
    )
```

```python
import jax
import jax.numpy as jnp
from jax import lax
from jax.sharding import PartitionSpec as P

BF16 = jnp.bfloat16
F32 = jnp.float32


def swiglu_grads(gate_pre, up_pre, hidden_grad):
    sigmoid_gate = jax.nn.sigmoid(gate_pre)
    activated = gate_pre * sigmoid_gate
    hidden = (activated * up_pre).astype(BF16)
    up_grad = (hidden_grad * activated).astype(BF16)
    slope = sigmoid_gate * (1.0 + gate_pre * (1.0 - sigmoid_gate))
    gate_grad = (hidden_grad * up_pre * slope).astype(BF16)
    return (gate_grad, up_grad, hidden)


def dot(first, second):
    return jnp.dot(first, second, preferred_element_type=F32)


def contract_rows(first, second):
    return lax.dot_general(
        first, second, (((0,), (0,)), ((), ())), preferred_element_type=F32
    )


def contract_cols(first, second):
    return lax.dot_general(
        first, second, (((1,), (1,)), ((), ())), preferred_element_type=F32
    )


def scatter_sum(parts, axis, groups):
    got = lax.all_to_all(parts, axis, 0, 0, tiled=True, axis_index_groups=groups)
    return jnp.sum(got.astype(F32), axis=0)


def gather(block, count, axis, groups):
    copies = jnp.broadcast_to(block[None], (count,) + block.shape)
    return lax.all_to_all(copies, axis, 0, 0, tiled=True, axis_index_groups=groups)


def per_device(ffn_input, attn_mix, out_grad, w_gate, w_up, w_down, w_out):
    rows, cols = lax.axis_size("row"), lax.axis_size("col")
    core = lax.axis_index("row") % 2
    seq = lax.axis_index("seq")
    tokens, width = ffn_input.shape
    hidden_width = w_gate.shape[1]
    half = tokens // 2
    chips = rows // 2
    share = half // chips
    core_swap = [(i, i ^ 1) for i in range(rows)]
    seq_swap = [(0, 1), (1, 0)]
    chip_groups = [list(range(c, rows, 2)) for c in range(2)]
    tie = lax.optimization_barrier
    near, far = 8, cols // 8

    def swap(x):
        return lax.ppermute(x, "row", core_swap)

    def halves(x):
        mine = lax.dynamic_slice_in_dim(x, core * half, half, 0)
        other = lax.dynamic_slice_in_dim(x, (1 - core) * half, half, 0)
        return mine, other

    in_mine, in_other = halves(ffn_input)
    out_mine, out_other = halves(out_grad)
    in_order = jnp.concatenate([in_mine, in_other])

    def products(x, g):
        blocks = [
            dot(a, w).astype(BF16).reshape(chips, share, hidden_width)
            for a, w in ((x, w_gate), (x, w_up), (g, w_down))
        ]
        return jnp.concatenate(blocks, axis=1)

    away = swap(products(in_other, out_other))
    parts = (products(in_mine, out_mine).astype(F32) + away.astype(F32)).astype(BF16)
    parts, w_gate, w_up, *to_swap = tie((parts, w_gate, w_up, w_out, out_other))
    w_both = jnp.concatenate([w_gate, w_up], axis=1)
    to_swap = [w_both, *to_swap]
    total = scatter_sum(parts, "row", chip_groups)
    w_both_far, w_out_far, out_far = (swap(x) for x in to_swap)
    w_out_pair = jnp.concatenate([w_out, w_out_far])
    out_pair = jnp.concatenate([out_mine, out_far], axis=1)
    spot = (lax.axis_index("col") + cols - 4 * core) % near
    out_piece = lax.dynamic_index_in_dim(out_pair.reshape(near, half // near, 2 * width), spot, 0, False)
    total, w_both_far, w_out_pair, out_piece, in_order = tie(
        (total, w_both_far, w_out_pair, out_piece, in_order)
    )
    gate_share, up_share, hid_share = swiglu_grads(
        total[:share], total[share : 2 * share], total[2 * share :]
    )
    def double(x, bit, runs=1):
        got = lax.ppermute(x, "row", [(i, i ^ bit) for i in range(rows)])
        low = (lax.axis_index("row") & bit) == 0
        x, got = (a.reshape(runs, -1, hidden_width) for a in (x, got))
        pair = jnp.where(low, jnp.concatenate([x, got], axis=1), jnp.concatenate([got, x], axis=1))
        return pair.reshape(-1, hidden_width)

    mine = gather(jnp.concatenate([gate_share, up_share], axis=1), chips, "row", chip_groups)
    mine, hid_pair = tie((mine.reshape(half, 2 * hidden_width), double(hid_share, 2)))

    def place(r, k, j):
        return r * cols + (k * near + j + 4 * (r % 2)) % cols

    near_groups = [[place(r, k, j) for j in range(near)] for r in range(rows) for k in range(far)]
    far_groups = [[place(r, k, j) for k in range(far)] for r in range(rows) for j in range(near)]
    both = ("row", "col")

    back_part = jnp.concatenate([contract_cols(mine, w).astype(BF16) for w in (w_both, w_both_far)], axis=1)
    back_part = back_part.reshape(near, half // near, 2 * width)
    back_part, sent_mine, hid_pair = tie((back_part, mine, hid_pair))
    other = swap(sent_mine)
    hid_row = double(hid_pair, 8)
    near_sum = scatter_sum(back_part, both, near_groups).astype(BF16)
    near_sum, other, hid_row = tie((near_sum, other, hid_row))

    norm_factor = (tokens * lax.axis_size("seq")) ** (-0.5)

    def wgrad(pairs, which, start=0, size=hidden_width // 2):
        terms = [
            contract_rows(a, lax.dynamic_slice_in_dim(b, start + which * size, size, 1))
            for a, b in pairs
        ]
        return sum(terms) * norm_factor

    both_pairs = ((in_order, jnp.concatenate([mine, other])),)
    sent = jnp.concatenate([wgrad(both_pairs, 1 - seq, n).astype(BF16) for n in (0, hidden_width)])
    received = lax.ppermute(sent, "seq", seq_swap)
    hid_row, _ = tie((hid_row, sent))
    hid_chips, received = tie((double(hid_row, 4, 2), received))
    hid_all = double(hid_chips, 1)

    group_sums = gather(near_sum, far, both, far_groups)
    far_sum = jnp.sum(group_sums.astype(F32), axis=0)
    gate_wgrad = wgrad(both_pairs, seq) + received[:width].astype(F32)
    up_wgrad = wgrad(both_pairs, seq, hidden_width) + received[width:].astype(F32)
    far_sum, hid_all = tie((far_sum, hid_all))
    resid_piece = (out_piece.astype(F32) + far_sum).astype(BF16)
    down_pairs = ((out_grad, hid_all),)
    down_received = lax.ppermute(wgrad(down_pairs, 1 - seq).astype(BF16), "seq", seq_swap)
    resid_all = gather(resid_piece, near, both, near_groups)
    resid_all, down_received, gate_wgrad, up_wgrad = tie(
        (resid_all, down_received, gate_wgrad, up_wgrad)
    )
    down_wgrad = wgrad(down_pairs, seq) + down_received.astype(F32)
    resid_all = resid_all.reshape(half, 2 * width)
    resid_mine, resid_far = resid_all[:, :width], resid_all[:, width:]

    def heads_by_tokens(w, x):
        return lax.dot_general(w, x, (((0,), (1,)), ((), ())), preferred_element_type=F32)

    mix_part = heads_by_tokens(w_out_pair, resid_all).astype(BF16)
    mix_part, resid_far = tie((mix_part, resid_far))
    mix_share = scatter_sum(mix_part.reshape(chips, -1, half), "row", chip_groups)
    mix_share, down_wgrad = tie((mix_share.astype(BF16), down_wgrad))
    mix_all = gather(mix_share, rows, "row", None)
    attn_grad = mix_all.reshape(chips, 2, -1, half).transpose(1, 3, 0, 2).reshape(tokens, -1)

    resid_other = swap(resid_far)
    resid_grad = jnp.where(
        core == 0,
        jnp.concatenate([resid_mine, resid_other]),
        jnp.concatenate([resid_other, resid_mine]),
    )
    out_pairs = ((resid_grad, attn_mix),)
    heads = attn_mix.shape[1] // 2
    out_sent = wgrad(out_pairs, 1 - seq, 0, heads).astype(BF16)
    out_wgrad = wgrad(out_pairs, seq, 0, heads) + lax.ppermute(out_sent, "seq", seq_swap).astype(F32)
    return (resid_grad, attn_grad, gate_wgrad, up_wgrad, down_wgrad, out_wgrad)


def solution(mesh):
    return jax.shard_map(
        per_device,
        mesh=mesh,
        in_specs=(
            P("seq", "row"),
            P("seq", "col"),
            P("seq", "row"),
            P("row", "col"),
            P("row", "col"),
            P("row", "col"),
            P("row", "col"),
        ),
        out_specs=(
            P("seq", "row"),
            P("seq", "col"),
            P("row", ("col", "seq")),
            P("row", ("col", "seq")),
            P("row", ("col", "seq")),
            P("row", ("col", "seq")),
        ),
        check_vma=False,
    )
```
